32 devices in a mesh: groups: 2 (over x), ctx: 16 (over z, y, core).
Axes of the slice: x: 2, y: 2, z: 4, core: 2. Of those that a mesh axis runs over, the one named last changes fastest.
Arguments:
- queries: bfloat16 [4096, 2048], P(('groups', 'ctx')), parts along dimension 0, may hold values from -90 to 90
- keys: bfloat16 [4096, 128], P(('groups', 'ctx')), parts along dimension 0, may hold values from -6 to 6
- values: bfloat16 [4096, 128], P(('groups', 'ctx')), parts along dimension 0, may hold values from -6 to 6
- cache_lengths: int32 [16], P('groups'), parts along dimension 0, may hold values from 1 to 1024, as said below
- query_lengths: int32 [16], P('groups'), parts along dimension 0, may hold values from 1 to 1024, as said below
Outputs:
- attended: bfloat16 [4096, 2048], P(('groups', 'ctx')), parts along dimension 0
- log_total: float32 [4096, 16], P(('groups', 'ctx')), parts along dimension 0
The draws below stay inside these ranges and needn't reach their ends.
There are 2 independent parts, one for each index of `groups`. The reference program is written for one: setup_inputs(seed, part) draws one part's arguments, and reference() takes and returns one part's arrays. A program takes and returns all parts, laid end to end along the dimension named above; each array names one. Nothing has to cross between parts.
Inputs may be any that keep to these rules, and one draw needn't show every extreme that they name: `cache_lengths`: Positive, summing to 2048; the largest is exactly 1024. `query_lengths`: Positive, summing to 2048; the largest is exactly 1024.
All inputs are finite; a program needn't handle non-finite values.
Results may differ from the reference program's by a relative error of at most 0.0045.
Values may be sent and summed in bfloat16 or wider, within the bound.
A program may use at most 64 MiB of HBM per device.

```python
import math
import jax
import jax.numpy as jnp
from jax import lax

HEADS = 16
DH = 128
REQUESTS = 8
QTOK = 2048
CTOK = 2048


def split_lengths(key, total, count):
    longest = total // 2
    rest = total - longest - (count - 1)
    cuts = jnp.sort(jax.random.randint(jax.random.fold_in(key, 1), (count - 2,), 0, rest + 1))
    edges = jnp.concatenate([jnp.zeros((1,), jnp.int32), cuts.astype(jnp.int32), jnp.full((1,), rest, jnp.int32)])
    pieces = jnp.diff(edges) + 1
    whole = jnp.concatenate([jnp.full((1,), longest, jnp.int32), pieces.astype(jnp.int32)])
    return jax.random.permutation(jax.random.fold_in(key, 2), whole)


def draw_cache_lengths(key, part):
    return split_lengths(jax.random.fold_in(key, 101), CTOK, REQUESTS)


def draw_query_lengths(key, part):
    return split_lengths(jax.random.fold_in(key, 202), QTOK, REQUESTS)


def key_table(key):
    return jnp.clip(jax.random.normal(jax.random.fold_in(key, 303), (CTOK, DH), jnp.float32), -6.0, 6.0)


def draw_keys(key, part):
    return key_table(key).astype(jnp.bfloat16)


def draw_queries(key, part):
    inner = jax.random.fold_in(key, 404)
    base = jnp.clip(jax.random.normal(inner, (QTOK, HEADS, DH), jnp.float32), -6.0, 6.0)
    return base.reshape(QTOK, HEADS * DH).astype(jnp.bfloat16)


def levels(rng, shape, split, least, high):
    loudness, own = 1.0, jax.random.fold_in(rng, 6)
    for position, parts in split:
        steps = jnp.exp(jax.random.uniform(jax.random.fold_in(own, position), (parts,), jnp.float32, least / len(split), high / len(split)))
        loudness = loudness * jnp.repeat(steps, shape[position] // parts).reshape([-1 if axis == position else 1 for axis in range(len(shape))])
    return loudness


def centred(own_key, dims, scale, most, cuts=(), kind=jnp.bfloat16):
    drawn = scale * jax.random.normal(own_key, dims, jnp.float32)
    if cuts:
        drawn = drawn * levels(own_key, dims, cuts, -0.22, 0.18)
    return jnp.clip(drawn, -most, most).astype(kind)


def setup_inputs(seed: int = 0, part: int = 0) -> dict:
    key_of = jax.random.split(jax.random.key(seed), 6)
    own_keys = jax.random.split(jax.random.fold_in(key_of[5], part), 6)
    return {
        "queries": draw_queries(jax.random.fold_in(jax.random.fold_in(key_of[5], part), 71), part),
        "keys": draw_keys(jax.random.fold_in(jax.random.fold_in(key_of[5], part), 71), part),
        "values": centred(own_keys[2], (CTOK, DH), 1.0, 6.0, ((0, 16),)),
        "cache_lengths": draw_cache_lengths(jax.random.fold_in(jax.random.fold_in(key_of[5], part), 71), part),
        "query_lengths": draw_query_lengths(jax.random.fold_in(jax.random.fold_in(key_of[5], part), 71), part),
    }


def request_of(positions, lengths):
    ends = jnp.cumsum(lengths)[:-1]
    return jnp.sum((positions[:, None] >= ends[None, :]).astype(jnp.int32), axis=1).astype(jnp.int32)


def reference(queries, keys, values, cache_lengths, query_lengths):
    qtok = queries.shape[0]
    ctok = keys.shape[0]
    cache_req = request_of(jnp.arange(ctok, dtype=jnp.int32), cache_lengths)
    query_req = request_of(jnp.arange(qtok, dtype=jnp.int32), query_lengths)
    block = math.gcd(qtok, 128)
    scale = DH ** -0.5
    keys_wide = keys.astype(jnp.float32)
    values_wide = values.astype(jnp.float32)
    query_blocks = queries.reshape(qtok // block, block, HEADS, DH)
    req_blocks = query_req.reshape(qtok // block, block)

    def one_block(item):
        qblock, rblock = item
        score = jnp.einsum("bhd,cd->bhc", qblock.astype(jnp.float32), keys_wide) * scale
        mask = rblock[:, None, None] == cache_req[None, None, :]
        score = jnp.where(mask, score, -1e30)
        top = jnp.max(score, axis=2)
        weight = jnp.where(mask, jnp.exp(score - top[:, :, None]), 0.0)
        total = jnp.sum(weight, axis=2)
        mixed = jnp.einsum("bhc,cd->bhd", weight.astype(jnp.bfloat16).astype(jnp.float32), values_wide)
        attended = (mixed / total[:, :, None]).astype(jnp.bfloat16)
        return attended, top + jnp.log(total)

    attended, log_total = lax.map(one_block, (query_blocks, req_blocks))
    return attended.reshape(qtok, HEADS * DH), log_total.reshape(qtok, HEADS)
```

```python
import functools
import math

import jax
import jax.numpy as jnp
from jax import lax
from jax.experimental import pallas as pl
from jax.experimental.pallas import tpu as pltpu
from jax.sharding import PartitionSpec as P

MESH = pl.DeviceIdType.MESH
APART = -(2.0**100)
LOWEST = -(2.0**90)
ROWS = 512


def flip(index, mask):
    out, bit = index, 1
    while bit <= mask:
        if mask & bit:
            out = out + bit - 2 * bit * lax.rem(lax.div(index, bit), 2)
        bit *= 2
    return out


def bounds(lengths_ref, lane):
    count = lengths_ref.shape[0]
    first = jnp.full(lane.shape, 2**30, jnp.int32)
    last = jnp.full(lane.shape, 2**30, jnp.int32)
    at = jnp.int32(0)
    for r in range(count):
        first = jnp.where(lane == r, at, first)
        at = at + lengths_ref[r]
        if r < count - 1:
            last = jnp.where(lane == r, at, last)
    return first, last


def kernel(n, q_hbm, k_hbm, v_hbm, clen, qlen, out_ref, log_ref,
           qbuf, kbuf, vbuf, acc, top, local_sem, send_sem, recv_sem):
    me = lax.axis_index("ctx")
    tokens, block = out_ref.shape[0], k_hbm.shape[0]
    width = k_hbm.shape[1]
    heads = out_ref.shape[1] // width
    count = clen.shape[0]
    zs = n // 4
    peers = [1, 2] + [4 * k for k in range(1, zs)]

    barrier = pltpu.get_barrier_semaphore()
    for j in peers:
        pl.semaphore_signal(barrier, inc=1, device_id={"ctx": flip(me, j)}, device_id_type=MESH)
    own_k = pltpu.make_async_copy(k_hbm, kbuf.at[0:block, 0:width], local_sem.at[0])
    own_v = pltpu.make_async_copy(v_hbm, vbuf.at[0:block, 0:width], local_sem.at[1])
    own_k.start()
    own_v.start()
    own_q = []
    for h in range(heads):
        copy = pltpu.make_async_copy(
            q_hbm.at[:, h * width:(h + 1) * width],
            qbuf.at[h * tokens:(h + 1) * tokens, 0:width],
            local_sem.at[2 + h])
        copy.start()
        own_q.append(copy)
    own_k.wait()
    own_v.wait()
    pl.semaphore_wait(barrier, len(peers))

    sends = []

    def send(slot, hop):
        to = slot ^ hop
        for i, buf in enumerate((kbuf, vbuf)):
            copy = pltpu.make_async_remote_copy(
                src_ref=buf.at[slot * block:(slot + 1) * block, 0:width],
                dst_ref=buf.at[to * block:(to + 1) * block, 0:width],
                send_sem=send_sem.at[i, to],
                recv_sem=recv_sem.at[i, to],
                device_id={"ctx": flip(me, hop)},
                device_id_type=MESH)
            copy.start()
            sends.append(copy)

    def arrived(slot):
        for i, buf in enumerate((kbuf, vbuf)):
            there = buf.at[slot * block:(slot + 1) * block, 0:width]
            pltpu.make_async_remote_copy(
                src_ref=there, dst_ref=there,
                send_sem=send_sem.at[i, slot], recv_sem=recv_sem.at[i, slot],
                device_id={"ctx": flip(me, 1)}, device_id_type=MESH).wait_recv()

    for j in peers:
        send(0, j)

    lane = lax.broadcasted_iota(jnp.int32, (1, width), 1)
    q_first, q_last = bounds(qlen, lane)
    k_first, k_last = bounds(clen, lane)
    row = lax.broadcasted_iota(jnp.int32, (tokens, width), 0) + me * tokens
    inside = (row >= q_first) & (row < q_last)
    apart = jnp.where(inside | (lane >= count), 0.0, APART).astype(jnp.bfloat16)
    for h in range(heads):
        qbuf[h * tokens:(h + 1) * tokens, width:] = apart
    vbuf[:, width:] = jnp.ones((n * block, width), jnp.bfloat16)
    spot = lax.broadcasted_iota(jnp.int32, (block, width), 0)
    for j in range(n):
        key = spot + flip(me, j) * block
        kbuf[j * block:(j + 1) * block, width:] = jnp.where(
            (key >= k_first) & (key < k_last), 1.0, 0.0).astype(jnp.bfloat16)
    for copy in own_q:
        copy.wait()

    factor2 = math.log2(math.e) * width ** -0.5
    span = 4 * block

    def attend(phase):
        keys = kbuf[phase * span:(phase + 1) * span, :]
        values = vbuf[phase * span:(phase + 1) * span, :]

        def rows(i, _):
            at = pl.ds(pl.multiple_of(i * ROWS, ROWS), ROWS)
            score = lax.dot_general(qbuf[at, :], keys, (((1,), (1,)), ((), ())),
                                    preferred_element_type=jnp.float32)
            most = jnp.max(score, axis=1, keepdims=True)
            if phase == 0:
                new = jnp.maximum(most, LOWEST)
            else:
                old = top[at, :]
                new = jnp.maximum(old[:, 0:1], most)
            weight = jnp.exp2((score - new) * factor2).astype(jnp.bfloat16)
            mixed = jnp.dot(weight, values, preferred_element_type=jnp.float32)
            if phase > 0:
                less = jnp.exp2((old - new) * factor2)
                mixed = jnp.concatenate([acc[at, 0:width] * less, acc[at, width:] * less], axis=1) + mixed
            acc[at, :] = mixed
            top[at, :] = jnp.broadcast_to(new, (ROWS, width))
            return 0

        lax.fori_loop(0, heads * tokens // ROWS, rows, 0)

    def forward(k):
        arrived(4 * k)
        send(4 * k, 2)
        send(4 * k, 1)

    def share(k):
        arrived(4 * k + 2)
        send(4 * k + 2, 1)

    share(0)
    if zs > 1:
        forward(1)
    for k in range(zs):
        arrived(4 * k + 1)
        arrived(4 * k + 3)
        if k + 1 < zs:
            share(k + 1)
        if k + 2 < zs:
            forward(k + 2)
        attend(k)

    logs = jnp.zeros((tokens, heads), jnp.float32)
    head_lane = lax.broadcasted_iota(jnp.int32, (tokens, heads), 1)
    for h in range(heads):
        at = slice(h * tokens, (h + 1) * tokens)
        total = acc[at, width:]
        out_ref[:, h * width:(h + 1) * width] = (acc[at, 0:width] / total).astype(jnp.bfloat16)
        log = top[at, 0:1] * (width ** -0.5) + jnp.log(total[:, 0:1])
        logs = jnp.where(head_lane == h, log, logs)
    log_ref[...] = logs
    for copy in sends:
        copy.wait_send()


def shards(n, queries, keys, values, cache_lengths, query_lengths):
    tokens, flat = queries.shape
    block, width = keys.shape
    heads = flat // width
    return pl.pallas_call(
        functools.partial(kernel, n),
        out_shape=(jax.ShapeDtypeStruct((tokens, flat), jnp.bfloat16),
                   jax.ShapeDtypeStruct((tokens, heads), jnp.float32)),
        in_specs=[pl.BlockSpec(memory_space=pl.ANY)] * 3 + [pl.BlockSpec(memory_space=pltpu.SMEM)] * 2,
        out_specs=(pl.BlockSpec(memory_space=pltpu.VMEM),) * 2,
        scratch_shapes=[
            pltpu.VMEM((heads * tokens, 2 * width), jnp.bfloat16),
            pltpu.VMEM((n * block, 2 * width), jnp.bfloat16),
            pltpu.VMEM((n * block, 2 * width), jnp.bfloat16),
            pltpu.VMEM((heads * tokens, 2 * width), jnp.float32),
            pltpu.VMEM((heads * tokens, width), jnp.float32),
            pltpu.SemaphoreType.DMA((2 + heads,)),
            pltpu.SemaphoreType.DMA((2, n)),
            pltpu.SemaphoreType.DMA((2, n)),
        ],
        compiler_params=pltpu.CompilerParams(
            collective_id=0, has_side_effects=True, vmem_limit_bytes=48 * 2**20),
        cost_estimate=pl.CostEstimate(
            flops=4 * heads * tokens * n * block * width,
            bytes_accessed=4 * tokens * flat + 4 * block * width,
            transcendentals=heads * tokens * n * block),
    )(queries, keys, values, cache_lengths, query_lengths)


def solution(mesh):
    in_specs = (
        P(("groups", "ctx"), None),
        P(("groups", "ctx"), None),
        P(("groups", "ctx"), None),
        P("groups"),
        P("groups"),
    )
    out_specs = (P(("groups", "ctx"), None), P(("groups", "ctx"), None))
    body = functools.partial(shards, mesh.shape["ctx"])
    return jax.shard_map(body, mesh=mesh, in_specs=in_specs, out_specs=out_specs, check_vma=False)
```

```python
import functools
import math

import jax
import jax.numpy as jnp
from jax import lax
from jax.experimental import pallas as pl
from jax.experimental.pallas import tpu as pltpu
from jax.sharding import PartitionSpec as P

MESH = pl.DeviceIdType.MESH
APART = -(2.0**100)
LOWEST = -(2.0**90)
ROWS = 2048
SPAN = 256
GVM = 63
AVM = 63


def flip(index, mask):
    out, bit = index, 1
    while bit <= mask:
        if mask & bit:
            out = out + bit - 2 * bit * lax.rem(lax.div(index, bit), 2)
        bit *= 2
    return out


def gather_kernel(n, k_hbm, v_hbm, k_all, v_all, local_sem, send_sem, recv_sem):
    me = lax.axis_index("ctx")
    block = k_hbm.shape[0]
    zs = n // 4
    K, V = 0, 1
    ins, outs = (k_hbm, v_hbm), (k_all, v_all)
    peers = [1, 2] + [4 * k for k in range(1, zs)]

    barrier = pltpu.get_barrier_semaphore()
    for j in peers:
        pl.semaphore_signal(barrier, inc=1, device_id={"ctx": flip(me, j)}, device_id_type=MESH)

    def place(i, j):
        at = pl.multiple_of(flip(me, j) * block, block)
        return outs[i].at[pl.ds(at, block), :]

    own = [pltpu.make_async_copy(ins[i], place(i, 0), local_sem.at[i]) for i in (K, V)]
    for copy in own:
        copy.start()
    pl.semaphore_wait(barrier, len(peers))

    sends = []

    def send(i, j, hop):
        copy = pltpu.make_async_remote_copy(
            src_ref=ins[i] if j == 0 else place(i, j),
            dst_ref=place(i, j),
            send_sem=send_sem.at[i, j ^ hop],
            recv_sem=recv_sem.at[i, j ^ hop],
            device_id={"ctx": flip(me, hop)},
            device_id_type=MESH)
        copy.start()
        sends.append(copy)

    def arrived(i, j):
        pltpu.make_async_remote_copy(
            src_ref=place(i, j), dst_ref=place(i, j),
            send_sem=send_sem.at[i, j], recv_sem=recv_sem.at[i, j],
            device_id={"ctx": flip(me, 1)}, device_id_type=MESH).wait_recv()

    send(V, 0, 2)
    for k in range(1, zs):
        send(K, 0, 4 * k)
    send(K, 0, 2)
    for k in range(1, zs):
        send(V, 0, 4 * k)
    send(K, 0, 1)
    send(V, 0, 1)
    arrived(V, 2)
    for k in range(1, zs):
        send(V, 2, 4 * k)
    send(V, 2, 1)
    for k in range(1, zs):
        arrived(K, 4 * k)
        send(K, 4 * k, 2)
        send(K, 4 * k, 1)
    arrived(K, 2)
    send(K, 2, 1)
    for k in range(1, zs):
        arrived(V, 4 * k)
        send(V, 4 * k, 1)
    for k in range(1, zs):
        arrived(V, 4 * k + 2)
        send(V, 4 * k + 2, 1)
        arrived(K, 4 * k + 2)
        send(K, 4 * k + 2, 1)
    for j in range(1, n, 2):
        arrived(K, j)
        arrived(V, j)
    for copy in own:
        copy.wait()
    for copy in sends:
        copy.wait_send()


def attend_kernel(q_hbm, k_hbm, v_hbm, clen, qlen, out_ref, log_ref,
                  qbuf, kbuf, vbuf, acc, top, sem):
    tokens, width, span = out_ref.shape[0], k_hbm.shape[1], SPAN
    length = k_hbm.shape[0]
    heads = out_ref.shape[1] // width
    count = clen.shape[0]
    start = lax.axis_index("ctx") * tokens

    copies = [pltpu.make_async_copy(k_hbm, kbuf.at[:, 0:width], sem.at[0]),
              pltpu.make_async_copy(v_hbm, vbuf.at[:, 0:width], sem.at[1])]
    for h in range(heads):
        copies.append(pltpu.make_async_copy(
            q_hbm.at[:, h * width:(h + 1) * width],
            qbuf.at[h * tokens:(h + 1) * tokens, 0:width], sem.at[2 + h]))
    for copy in copies:
        copy.start()

    lane = lax.broadcasted_iota(jnp.int32, (1, width), 1)
    big = jnp.full((1, width), 2**30, jnp.int32)
    q_first, q_last, k_first, k_last = big, big, big, big
    low, high = jnp.int32(length), jnp.int32(0)
    q_at, k_at = jnp.int32(0), jnp.int32(0)
    for r in range(count):
        q_end = q_at + qlen[r] if r < count - 1 else jnp.int32(2**30)
        k_end = k_at + clen[r] if r < count - 1 else jnp.int32(length)
        here = lane == r
        q_first, q_last = jnp.where(here, q_at, q_first), jnp.where(here, q_end, q_last)
        k_first, k_last = jnp.where(here, k_at, k_first), jnp.where(here, k_end, k_last)
        used = (q_at < start + tokens) & (q_end > start)
        low = jnp.where(used, jnp.minimum(low, k_at), low)
        high = jnp.where(used, jnp.maximum(high, k_end), high)
        q_at, k_at = q_end, k_end

    row = lax.broadcasted_iota(jnp.int32, (tokens, width), 0) + start
    inside = (row >= q_first) & (row < q_last)
    apart = jnp.where(inside | (lane >= count), 0.0, APART).astype(jnp.bfloat16)
    for h in range(heads):
        qbuf[h * tokens:(h + 1) * tokens, width:] = apart
    vbuf[:, width:] = jnp.ones((length, width), jnp.bfloat16)
    acc[...] = jnp.zeros(acc.shape, jnp.float32)
    top[...] = jnp.full(top.shape, LOWEST, jnp.float32)
    spot = lax.broadcasted_iota(jnp.int32, (span, width), 0)
    for copy in copies:
        copy.wait()
    factor2 = math.log2(math.e) * width ** -0.5

    def step(j, _):
        at = pl.ds(pl.multiple_of(j * span, span), span)
        key = spot + j * span
        mark = jnp.where((key >= k_first) & (key < k_last), 1.0, 0.0).astype(jnp.bfloat16)
        keys = jnp.concatenate([kbuf[at, 0:width], mark], axis=1)
        values = vbuf[at, :]
        for i in range(heads * tokens // ROWS):
            rows = slice(i * ROWS, (i + 1) * ROWS)
            score = lax.dot_general(qbuf[rows, :], keys, (((1,), (1,)), ((), ())),
                                    preferred_element_type=jnp.float32)
            old = top[rows, :]
            most = jnp.broadcast_to(jnp.max(score, axis=1, keepdims=True), old.shape)
            new = jnp.maximum(old, most)
            weight = jnp.concatenate(
                [jnp.exp2((score[:, c:c + width] - new) * factor2).astype(jnp.bfloat16)
                 for c in range(0, span, width)], axis=1)
            mixed = jnp.dot(weight, values, preferred_element_type=jnp.float32)
            less = jnp.exp2((old - new) * factor2)
            acc[rows, :] = jnp.concatenate([acc[rows, 0:width] * less, acc[rows, width:] * less], axis=1) + mixed
            top[rows, :] = new
        return 0

    lax.fori_loop(lax.div(low, span), lax.div(high + span - 1, span), step, 0)

    totals = jnp.ones((tokens, width), jnp.float32)
    tops = jnp.zeros((tokens, width), jnp.float32)
    for h in range(heads):
        rows = slice(h * tokens, (h + 1) * tokens)
        total = acc[rows, width:]
        out_ref[:, h * width:(h + 1) * width] = (acc[rows, 0:width] / total).astype(jnp.bfloat16)
        totals = jnp.where(lane == h, total, totals)
        tops = jnp.where(lane == h, top[rows, :], tops)
    logs = tops * (width ** -0.5) + jnp.log(totals)
    log_ref[...] = logs.T[0:heads, :]


def shards(n, queries, keys, values, cache_lengths, query_lengths):
    tokens, flat = queries.shape
    block, width = keys.shape
    heads = flat // width
    whole = jax.ShapeDtypeStruct((n * block, width), jnp.bfloat16)
    anywhere = pl.BlockSpec(memory_space=pl.ANY)
    k_all, v_all = pl.pallas_call(
        functools.partial(gather_kernel, n),
        out_shape=(whole, whole),
        in_specs=[anywhere] * 2,
        out_specs=(anywhere,) * 2,
        scratch_shapes=[
            pltpu.SemaphoreType.DMA((2,)),
            pltpu.SemaphoreType.DMA((2, n)),
            pltpu.SemaphoreType.DMA((2, n)),
        ],
        compiler_params=pltpu.CompilerParams(
            collective_id=0, has_side_effects=True, vmem_limit_bytes=GVM * 2**20),
    )(keys, values)
    attended, log_total = pl.pallas_call(
        attend_kernel,
        out_shape=(jax.ShapeDtypeStruct((tokens, flat), jnp.bfloat16),
                   jax.ShapeDtypeStruct((heads, tokens), jnp.float32)),
        in_specs=[anywhere] * 3 + [pl.BlockSpec(memory_space=pltpu.SMEM)] * 2,
        out_specs=(pl.BlockSpec(memory_space=pltpu.VMEM),) * 2,
        scratch_shapes=[
            pltpu.VMEM((heads * tokens, 2 * width), jnp.bfloat16),
            pltpu.VMEM((n * block, 2 * width), jnp.bfloat16),
            pltpu.VMEM((n * block, 2 * width), jnp.bfloat16),
            pltpu.VMEM((heads * tokens, 2 * width), jnp.float32),
            pltpu.VMEM((heads * tokens, width), jnp.float32),
            pltpu.SemaphoreType.DMA((2 + heads,)),
        ],
        compiler_params=pltpu.CompilerParams(vmem_limit_bytes=AVM * 2**20),
        cost_estimate=pl.CostEstimate(
            flops=4 * heads * tokens * n * block * width,
            bytes_accessed=4 * tokens * flat + 4 * block * width,
            transcendentals=heads * tokens * n * block),
    )(queries, k_all, v_all, cache_lengths, query_lengths)
    return attended, log_total.T


def solution(mesh):
    in_specs = (
        P(("groups", "ctx"), None),
        P(("groups", "ctx"), None),
        P(("groups", "ctx"), None),
        P("groups"),
        P("groups"),
    )
    out_specs = (P(("groups", "ctx"), None), P(("groups", "ctx"), None))
    body = functools.partial(shards, mesh.shape["ctx"])
    return jax.shard_map(body, mesh=mesh, in_specs=in_specs, out_specs=out_specs, check_vma=False)
```

```python
import functools
import math

import jax
import jax.numpy as jnp
from jax import lax
from jax.experimental import pallas as pl
from jax.experimental.pallas import tpu as pltpu
from jax.sharding import PartitionSpec as P

MESH = pl.DeviceIdType.MESH
APART = -(2.0**100)
LOWEST = -(2.0**90)
ROWS = 2048
SPAN = 256
GVM = 63
AVM = 63


def flip(index, mask):
    out, bit = index, 1
    while bit <= mask:
        if mask & bit:
            out = out + bit - 2 * bit * lax.rem(lax.div(index, bit), 2)
        bit *= 2
    return out


def gather_kernel(n, k_hbm, v_hbm, k_all, v_all, local_sem, send_sem, recv_sem):
    me = lax.axis_index("ctx")
    block = k_hbm.shape[0]
    zs = n // 4
    K, V = 0, 1
    ins, outs = (k_hbm, v_hbm), (k_all, v_all)
    peers = [1, 2] + [4 * k for k in range(1, zs)]

    barrier = pltpu.get_barrier_semaphore()
    for j in peers:
        pl.semaphore_signal(barrier, inc=1, device_id={"ctx": flip(me, j)}, device_id_type=MESH)

    def place(i, j):
        at = pl.multiple_of(flip(me, j) * block, block)
        return outs[i].at[pl.ds(at, block), :]

    own = [pltpu.make_async_copy(ins[i], place(i, 0), local_sem.at[i]) for i in (K, V)]
    for copy in own:
        copy.start()
    pl.semaphore_wait(barrier, len(peers))

    sends = []

    def send(i, j, hop):
        copy = pltpu.make_async_remote_copy(
            src_ref=ins[i] if j == 0 else place(i, j),
            dst_ref=place(i, j),
            send_sem=send_sem.at[i, j ^ hop],
            recv_sem=recv_sem.at[i, j ^ hop],
            device_id={"ctx": flip(me, hop)},
            device_id_type=MESH)
        copy.start()
        sends.append(copy)

    def arrived(i, j):
        pltpu.make_async_remote_copy(
            src_ref=place(i, j), dst_ref=place(i, j),
            send_sem=send_sem.at[i, j], recv_sem=recv_sem.at[i, j],
            device_id={"ctx": flip(me, 1)}, device_id_type=MESH).wait_recv()

    send(V, 0, 2)
    for k in range(1, zs):
        send(K, 0, 4 * k)
    send(K, 0, 2)
    for k in range(1, zs):
        send(V, 0, 4 * k)
    send(K, 0, 1)
    send(V, 0, 1)
    arrived(V, 2)
    for k in range(1, zs):
        send(V, 2, 4 * k)
    send(V, 2, 1)
    for k in range(1, zs):
        arrived(K, 4 * k)
        send(K, 4 * k, 2)
        send(K, 4 * k, 1)
    arrived(K, 2)
    send(K, 2, 1)
    for k in range(1, zs):
        arrived(V, 4 * k)
        send(V, 4 * k, 1)
    for k in range(1, zs):
        arrived(V, 4 * k + 2)
        send(V, 4 * k + 2, 1)
        arrived(K, 4 * k + 2)
        send(K, 4 * k + 2, 1)
    for j in range(1, n, 2):
        arrived(K, j)
        arrived(V, j)
    for copy in own:
        copy.wait()
    for copy in sends:
        copy.wait_send()


def attend_kernel(q_hbm, k_hbm, v_hbm, clen, qlen, out_ref, log_ref,
                  qbuf, kbuf, vbuf, acc, top, sem):
    tokens, width, span = out_ref.shape[0], k_hbm.shape[1], SPAN
    length = k_hbm.shape[0]
    heads = out_ref.shape[1] // width
    count = clen.shape[0]
    start = lax.axis_index("ctx") * tokens

    copies = [pltpu.make_async_copy(k_hbm, kbuf.at[:, 0:width], sem.at[0]),
              pltpu.make_async_copy(v_hbm, vbuf.at[:, 0:width], sem.at[1])]
    for h in range(heads):
        copies.append(pltpu.make_async_copy(
            q_hbm.at[:, h * width:(h + 1) * width],
            qbuf.at[h * tokens:(h + 1) * tokens, 0:width], sem.at[2 + h]))
    for copy in copies:
        copy.start()

    lane = lax.broadcasted_iota(jnp.int32, (1, width), 1)
    big = jnp.full((1, width), 2**30, jnp.int32)
    q_first, q_last, k_first, k_last = big, big, big, big
    low, high = jnp.int32(length), jnp.int32(0)
    q_at, k_at = jnp.int32(0), jnp.int32(0)
    for r in range(count):
        q_end = q_at + qlen[r] if r < count - 1 else jnp.int32(2**30)
        k_end = k_at + clen[r] if r < count - 1 else jnp.int32(length)
        here = lane == r
        q_first, q_last = jnp.where(here, q_at, q_first), jnp.where(here, q_end, q_last)
        k_first, k_last = jnp.where(here, k_at, k_first), jnp.where(here, k_end, k_last)
        used = (q_at < start + tokens) & (q_end > start)
        low = jnp.where(used, jnp.minimum(low, k_at), low)
        high = jnp.where(used, jnp.maximum(high, k_end), high)
        q_at, k_at = q_end, k_end

    row = lax.broadcasted_iota(jnp.int32, (tokens, width), 0) + start
    inside = (row >= q_first) & (row < q_last)
    apart = jnp.where(inside | (lane >= count), 0.0, APART).astype(jnp.bfloat16)
    for h in range(heads):
        qbuf[h * tokens:(h + 1) * tokens, width:] = apart
    vbuf[:, width:] = jnp.ones((length, width), jnp.bfloat16)
    acc[...] = jnp.zeros(acc.shape, jnp.float32)
    top[...] = jnp.full(top.shape, LOWEST, jnp.float32)
    spot = lax.broadcasted_iota(jnp.int32, (span, width), 0)
    for copy in copies:
        copy.wait()
    factor2 = math.log2(math.e) * width ** -0.5

    def step(j, _):
        begin = base + j * span
        at = jnp.minimum(begin, length - span)
        key = spot + at
        at = pl.ds(pl.multiple_of(at, 16), span)
        marked = ((key >= k_first) & (key < k_last)) | (key < begin)
        mark = jnp.where(marked, 1.0, 0.0).astype(jnp.bfloat16)
        keys = jnp.concatenate([kbuf[at, 0:width], mark], axis=1)
        values = vbuf[at, :]
        for i in range(heads * tokens // ROWS):
            rows = slice(i * ROWS, (i + 1) * ROWS)
            score = lax.dot_general(qbuf[rows, :], keys, (((1,), (1,)), ((), ())),
                                    preferred_element_type=jnp.float32)
            old = top[rows, :]
            most = jnp.broadcast_to(jnp.max(score, axis=1, keepdims=True), old.shape)
            new = jnp.maximum(old, most)
            weight = jnp.concatenate(
                [jnp.exp2((score[:, c:c + width] - new) * factor2).astype(jnp.bfloat16)
                 for c in range(0, span, width)], axis=1)
            mixed = jnp.dot(weight, values, preferred_element_type=jnp.float32)
            less = jnp.exp2((old - new) * factor2)
            acc[rows, :] = jnp.concatenate([acc[rows, 0:width] * less, acc[rows, width:] * less], axis=1) + mixed
            top[rows, :] = new
        return 0

    base = lax.div(low, 16) * 16
    lax.fori_loop(0, lax.div(high - base + span - 1, span), step, 0)

    totals = jnp.ones((tokens, width), jnp.float32)
    tops = jnp.zeros((tokens, width), jnp.float32)
    for h in range(heads):
        rows = slice(h * tokens, (h + 1) * tokens)
        total = acc[rows, width:]
        out_ref[:, h * width:(h + 1) * width] = (acc[rows, 0:width] / total).astype(jnp.bfloat16)
        totals = jnp.where(lane == h, total, totals)
        tops = jnp.where(lane == h, top[rows, :], tops)
    logs = tops * (width ** -0.5) + jnp.log(totals)
    log_ref[...] = logs.T[0:heads, :]


def shards(n, queries, keys, values, cache_lengths, query_lengths):
    tokens, flat = queries.shape
    block, width = keys.shape
    heads = flat // width
    whole = jax.ShapeDtypeStruct((n * block, width), jnp.bfloat16)
    anywhere = pl.BlockSpec(memory_space=pl.ANY)
    k_all, v_all = pl.pallas_call(
        functools.partial(gather_kernel, n),
        out_shape=(whole, whole),
        in_specs=[anywhere] * 2,
        out_specs=(anywhere,) * 2,
        scratch_shapes=[
            pltpu.SemaphoreType.DMA((2,)),
            pltpu.SemaphoreType.DMA((2, n)),
            pltpu.SemaphoreType.DMA((2, n)),
        ],
        compiler_params=pltpu.CompilerParams(
            collective_id=0, has_side_effects=True, vmem_limit_bytes=GVM * 2**20),
    )(keys, values)
    attended, log_total = pl.pallas_call(
        attend_kernel,
        out_shape=(jax.ShapeDtypeStruct((tokens, flat), jnp.bfloat16),
                   jax.ShapeDtypeStruct((heads, tokens), jnp.float32)),
        in_specs=[anywhere] * 3 + [pl.BlockSpec(memory_space=pltpu.SMEM)] * 2,
        out_specs=(pl.BlockSpec(memory_space=pltpu.VMEM),) * 2,
        scratch_shapes=[
            pltpu.VMEM((heads * tokens, 2 * width), jnp.bfloat16),
            pltpu.VMEM((n * block, 2 * width), jnp.bfloat16),
            pltpu.VMEM((n * block, 2 * width), jnp.bfloat16),
            pltpu.VMEM((heads * tokens, 2 * width), jnp.float32),
            pltpu.VMEM((heads * tokens, width), jnp.float32),
            pltpu.SemaphoreType.DMA((2 + heads,)),
        ],
        compiler_params=pltpu.CompilerParams(vmem_limit_bytes=AVM * 2**20),
        cost_estimate=pl.CostEstimate(
            flops=4 * heads * tokens * n * block * width,
            bytes_accessed=4 * tokens * flat + 4 * block * width,
            transcendentals=heads * tokens * n * block),
    )(queries, k_all, v_all, cache_lengths, query_lengths)
    return attended, log_total.T


def solution(mesh):
    in_specs = (
        P(("groups", "ctx"), None),
        P(("groups", "ctx"), None),
        P(("groups", "ctx"), None),
        P("groups"),
        P("groups"),
    )
    out_specs = (P(("groups", "ctx"), None), P(("groups", "ctx"), None))
    body = functools.partial(shards, mesh.shape["ctx"])
    return jax.shard_map(body, mesh=mesh, in_specs=in_specs, out_specs=out_specs, check_vma=False)
```
